32 devices in a mesh: dp: 16 (over z, y, x), tensor: 2 (over core).
Axes of the slice: x: 2, y: 2, z: 4, core: 2. Of those that a mesh axis runs over, the one named last changes fastest.
Arguments:
- tokens: bfloat16 [16384, 1024], P('dp'), may hold values from -6 to 6
- norm_gain: float32 [1024], replicated, may hold values from 0.5 to 1.5
- z_proj: bfloat16 [1024, 2048], P(None, 'tensor'), may hold values from -0.1875 to 0.1875
- x_proj: bfloat16 [1024, 2048], P(None, 'tensor'), may hold values from -0.1875 to 0.1875
- dt_proj: bfloat16 [1024, 32], P(None, 'tensor'), may hold values from -0.1875 to 0.1875
- bc_proj: bfloat16 [1024, 256], replicated, may hold values from -0.1875 to 0.1875
- x_conv: float32 [4, 2048], P(None, 'tensor'), may hold values from -1.5 to 1.5
- x_conv_bias: float32 [2048], P('tensor'), may hold values from -1 to 1
- bc_conv: float32 [4, 256], replicated, may hold values from -1.5 to 1.5
- bc_conv_bias: float32 [256], replicated, may hold values from -1 to 1
- dt_bias: float32 [32], P('tensor'), may hold values from -4.6 to -2.3
- a_log: float32 [32], P('tensor'), may hold values from 0 to 2.77
- d_skip: float32 [32], P('tensor'), may hold values from 0.5 to 1.5
- gate_gain: float32 [2048], P('tensor'), may hold values from 0.5 to 1.5
- out_proj: bfloat16 [2048, 1024], P('tensor'), may hold values from -0.125 to 0.125
- cotangent: bfloat16 [16384, 1024], P('dp'), may hold values from -6 to 6
Outputs:
- mixed: bfloat16 [16384, 1024], P('dp')
- tokens_grad: bfloat16 [16384, 1024], P('dp')
- norm_gain_grad: float32 [1024], replicated
- z_proj_grad: float32 [1024, 2048], P(None, 'tensor')
- x_proj_grad: float32 [1024, 2048], P(None, 'tensor')
- dt_proj_grad: float32 [1024, 32], P(None, 'tensor')
- bc_proj_grad: float32 [1024, 256], replicated
- x_conv_grad: float32 [4, 2048], P(None, 'tensor')
- x_conv_bias_grad: float32 [2048], P('tensor')
- bc_conv_grad: float32 [4, 256], replicated
- bc_conv_bias_grad: float32 [256], replicated
- dt_bias_grad: float32 [32], P('tensor')
- a_log_grad: float32 [32], P('tensor')
- d_skip_grad: float32 [32], P('tensor')
- gate_gain_grad: float32 [2048], P('tensor')
- out_proj_grad: float32 [2048, 1024], P('tensor')
The draws below stay inside these ranges and needn't reach their ends.
All inputs are finite; a program needn't handle non-finite values.
Results may differ from the reference program's by a relative error of at most 0.02.
Values may be sent and summed in bfloat16 or wider, within the bound.
A program may use at most 128 MiB of HBM per device.

```python
import jax
import jax.numpy as jnp
from jax import lax

D = 1024
INNER = 2048
HEADS = 32
STATE = 128
CONV = 4
STRETCH = 256
SEQ_LEN = 1024
TOK_DEV = 1024
TOKENS = 16384
N_DP = 16


def block_levels(key, dims, pieces, least, largest):
    factor_of = 1.0
    for dim, blocks in pieces:
        heights = jax.random.uniform(jax.random.fold_in(jax.random.fold_in(key, 6), dim), (blocks,), jnp.float32, least / len(pieces), largest / len(pieces))
        factor_of = factor_of * jnp.repeat(jnp.exp(heights), dims[dim] // blocks).reshape((-1,) + (1,) * (len(dims) - 1 - dim))
    return factor_of


def noise(rng, dims, spread, most, shards=(), kind=jnp.bfloat16):
    gain = block_levels(rng, dims, shards, -0.22, 0.18) if shards else 1.0
    values = jax.random.normal(rng, dims, jnp.float32) * spread * gain
    return jnp.minimum(jnp.maximum(values, -most), most).astype(kind)


def setup_inputs(seed: int = 0) -> dict:
    keys = jax.random.split(jax.random.key(seed), 17)
    tokens = noise(keys[0], (TOKENS, D), 1.0, 6.0, ((0, 16),))
    norm_gain = jnp.clip(1.0 + 0.1 * jax.random.normal(keys[1], (D,), jnp.float32), 0.5, 1.5)
    z_proj = noise(keys[2], (D, INNER), D ** -0.5, 0.1875, ((1, 2),))
    x_proj = noise(keys[3], (D, INNER), D ** -0.5, 0.1875, ((1, 2),))
    dt_proj = noise(keys[4], (D, HEADS), D ** -0.5, 0.1875, ((1, 2),))
    bc_proj = noise(keys[5], (D, 2 * STATE), D ** -0.5, 0.1875)
    x_conv = noise(keys[6], (CONV, INNER), 0.5, 1.5, ((1, 2),), jnp.float32)
    x_conv_bias = noise(keys[7], (INNER,), 0.3, 1.0, ((0, 2),), jnp.float32)
    bc_conv = noise(keys[8], (CONV, 2 * STATE), 0.5, 1.5, (), jnp.float32)
    bc_conv_bias = noise(keys[9], (2 * STATE,), 0.3, 1.0, (), jnp.float32)
    dt_bias = jnp.clip(-4.6 + 2.3 * jax.random.uniform(keys[10], (HEADS,), jnp.float32) ** block_levels(keys[10], (HEADS,), ((0, 2),), -0.2, 0.2), -4.6, -2.3)
    a_log = jnp.clip(2.77 * jax.random.uniform(keys[11], (HEADS,), jnp.float32) ** block_levels(keys[11], (HEADS,), ((0, 2),), -0.2, 0.2), 0.0, 2.77)
    d_skip = jnp.clip(0.5 + 1.0 * jax.random.uniform(keys[12], (HEADS,), jnp.float32) ** block_levels(keys[12], (HEADS,), ((0, 2),), -0.2, 0.2), 0.5, 1.5)
    gate_gain = jnp.clip(1.0 + 0.1 * jax.random.normal(keys[13], (INNER,), jnp.float32), 0.5, 1.5)
    out_proj = noise(keys[14], (INNER, D), INNER ** -0.5, 0.125, ((0, 2),))
    cotangent = noise(keys[15], (TOKENS, D), 1.0, 6.0, ((0, 16),))
    return {"tokens": tokens, "norm_gain": norm_gain, "z_proj": z_proj, "x_proj": x_proj, "dt_proj": dt_proj, "bc_proj": bc_proj, "x_conv": x_conv, "x_conv_bias": x_conv_bias, "bc_conv": bc_conv, "bc_conv_bias": bc_conv_bias, "dt_bias": dt_bias, "a_log": a_log, "d_skip": d_skip, "gate_gain": gate_gain, "out_proj": out_proj, "cotangent": cotangent}


EPS = 1e-05
HIGH = lax.Precision.HIGHEST

@jax.custom_vjp
def low(v):
    return lax.optimization_barrier(v.astype(jnp.bfloat16)).astype(jnp.float32)

@jax.custom_vjp
def low_back(v):
    return v

def low_keep(v):
    return (low(v), None)

def low_pass(kept, grad):
    return (grad,)

def back_keep(v):
    return (v, None)

def back_low(kept, grad):
    return (low(grad),)
low.defvjp(low_keep, low_pass)
low_back.defvjp(back_keep, back_low)

def matmul(left, right):
    return jnp.dot(left, right, precision=HIGH, preferred_element_type=jnp.float32)

def causal_conv(sequence, weights, offsets):
    row_count, channels = sequence.shape
    kernel_width = weights.shape[0]
    blocked = sequence.reshape(row_count // SEQ_LEN, SEQ_LEN, channels)
    padded = jnp.pad(blocked, ((0, 0), (kernel_width - 1, 0), (0, 0)))
    summed = jnp.zeros_like(blocked) + offsets
    for offset in range(kernel_width):
        summed = summed + weights[offset] * padded[:, offset:offset + SEQ_LEN]
    return jax.nn.silu(summed).reshape(row_count, channels)

def ssd_sequence(values, step_dt, decay_rates, input_b, output_c):
    length, head_count, head_dim = values.shape
    state_size = input_b.shape[1]
    block_count = length // STRETCH
    places = jnp.arange(STRETCH)
    lower_mask = (places[:, None] >= places[None, :])[:, :, None]

    def advance(inner_state, block_data):
        block_vals, block_dt, block_b, block_c = block_data
        cumulative = jnp.cumsum(block_dt * decay_rates, axis=0)
        spreads = jnp.where(lower_mask, cumulative[:, None, :] - cumulative[None, :, :], 0.0)
        decays = jnp.where(lower_mask, jnp.exp(spreads), 0.0)
        scores = jnp.dot(block_c, block_b.T, precision=HIGH)
        mixing = scores[:, :, None] * decays * block_dt[None, :, :]
        within = jnp.einsum('ijh,jhp->ihp', mixing, block_vals, precision=HIGH)
        carried = jnp.einsum('in,hpn->ihp', block_c, inner_state, precision=HIGH) * jnp.exp(cumulative)[:, :, None]
        tail_gain = jnp.exp(cumulative[-1][None, :] - cumulative) * block_dt
        arrival = jnp.einsum('jh,jn,jhp->hpn', tail_gain, block_b, block_vals, precision=HIGH)
        return (inner_state * jnp.exp(cumulative[-1])[:, None, None] + arrival, within + carried)
    initial = jnp.zeros((head_count, head_dim, state_size), jnp.float32)
    _, results = lax.scan(jax.checkpoint(advance), initial, (values.reshape(block_count, STRETCH, head_count, head_dim), step_dt.reshape(block_count, STRETCH, head_count), input_b.reshape(block_count, STRETCH, state_size), output_c.reshape(block_count, STRETCH, state_size)))
    return results.reshape(length, head_count, head_dim)

def mixer(z_pre, x_pre, dt_pre, bc_pre, x_conv, x_conv_bias, bc_conv, bc_conv_bias, dt_bias, a_log, d_skip):
    row_count = z_pre.shape[0]
    head_count = dt_pre.shape[1]
    head_dim = x_pre.shape[1] // head_count
    x_mixed = causal_conv(x_pre, x_conv, x_conv_bias)
    bc_mixed = causal_conv(bc_pre, bc_conv, bc_conv_bias)
    state_size = bc_mixed.shape[1] // 2
    step_dt = jax.nn.softplus(dt_pre + dt_bias)
    decay_rates = -jnp.exp(a_log)
    seq_count = row_count // SEQ_LEN
    values = x_mixed.reshape(seq_count, SEQ_LEN, head_count, head_dim)
    scanned = jax.vmap(ssd_sequence, in_axes=(0, 0, None, 0, 0))(values, step_dt.reshape(seq_count, SEQ_LEN, head_count), decay_rates, bc_mixed[:, :state_size].reshape(seq_count, SEQ_LEN, state_size), bc_mixed[:, state_size:].reshape(seq_count, SEQ_LEN, state_size))
    scanned = scanned + d_skip[:, None] * values
    return scanned.reshape(row_count, head_count * head_dim) * jax.nn.silu(z_pre)

def forward(hidden, norm_gain, z_proj, x_proj, dt_proj, bc_proj, x_conv, x_conv_bias, bc_conv, bc_conv_bias, dt_bias, a_log, d_skip, gate_gain, out_proj):
    inv_rms = lax.rsqrt(lax.optimization_barrier(jnp.mean(hidden * hidden, axis=1, keepdims=True)) + EPS)
    normed_in = low(hidden * inv_rms * norm_gain)
    z_pre = low_back(matmul(normed_in, z_proj))
    x_pre = low_back(matmul(normed_in, x_proj))
    dt_pre = low_back(matmul(normed_in, dt_proj))
    bc_pre = low_back(matmul(normed_in, bc_proj))
    gated = mixer(z_pre, x_pre, dt_pre, bc_pre, x_conv, x_conv_bias, bc_conv, bc_conv_bias, dt_bias, a_log, d_skip)
    gate_rms = lax.rsqrt(lax.optimization_barrier(jnp.mean(gated * gated, axis=1, keepdims=True)) + EPS)
    gate_out = low(gated * gate_rms * gate_gain)
    return hidden + matmul(gate_out, out_proj)

def reference(tokens, norm_gain, z_proj, x_proj, dt_proj, bc_proj, x_conv, x_conv_bias, bc_conv, bc_conv_bias, dt_bias, a_log, d_skip, gate_gain, out_proj, cotangent):
    params = tuple((weight.astype(jnp.float32) for weight in (norm_gain, z_proj, x_proj, dt_proj, bc_proj, x_conv, x_conv_bias, bc_conv, bc_conv_bias, dt_bias, a_log, d_skip, gate_gain, out_proj)))

    def one_group(totals, group):
        group_rows, group_cot = group
        result, pull = jax.vjp(forward, group_rows.astype(jnp.float32), *params)
        grads = pull(group_cot.astype(jnp.float32))
        added = tuple((earlier + fresh for earlier, fresh in zip(totals, grads[1:])))
        return (added, (result.astype(jnp.bfloat16), grads[0].astype(jnp.bfloat16)))
    zeros = tuple((jnp.zeros_like(weight) for weight in params))
    sums, (mixed, tokens_grad) = lax.scan(one_group, zeros, (tokens.reshape(N_DP, TOK_DEV, D), cotangent.reshape(N_DP, TOK_DEV, D)))
    return (mixed.reshape(TOKENS, D), tokens_grad.reshape(TOKENS, D), sums[0], sums[1], sums[2], sums[3], sums[4], sums[5], sums[6], sums[7], sums[8], sums[9], sums[10], sums[11], sums[12], sums[13])
```

```python
import jax
import jax.numpy as jnp
from jax import lax
from jax.experimental import pallas as pl
from jax.experimental.pallas import tpu as pltpu
from jax.sharding import PartitionSpec as P

INNER = 2048
STRETCH = 256
SEQ_LEN = 1024
EPS = 1e-05
HIGH = lax.Precision.HIGHEST
CHUNKS = SEQ_LEN // STRETCH
LANES = 128
F32 = jnp.float32
BF16 = jnp.bfloat16


def causal_conv(sequence, weights, offsets):
    row_count, channels = sequence.shape
    kernel_width = weights.shape[0]
    blocked = sequence.reshape(row_count // SEQ_LEN, SEQ_LEN, channels)
    padded = jnp.pad(blocked, ((0, 0), (kernel_width - 1, 0), (0, 0)))
    summed = jnp.zeros_like(blocked) + offsets
    for offset in range(kernel_width):
        summed = summed + weights[offset] * padded[:, offset : offset + SEQ_LEN]
    return jax.nn.silu(summed).reshape(row_count, channels)


def nn(left, right):
    return jnp.dot(left, right, preferred_element_type=F32)


def nt(left, right):
    return lax.dot_general(left, right, (((1,), (1,)), ((), ())), preferred_element_type=F32)


def tn(left, right):
    return lax.dot_general(left, right, (((0,), (0,)), ((), ())), preferred_element_type=F32)


def first_half(shape):
    return lax.broadcasted_iota(jnp.int32, shape, 1) < LANES // 2


def spread(pair):
    rows = pair.shape[0]
    return jnp.where(
        first_half((rows, LANES)),
        jnp.broadcast_to(pair[:, 0:1], (rows, LANES)),
        jnp.broadcast_to(pair[:, 1:2], (rows, LANES)),
    )


def head_sums(wide):
    first = first_half(wide.shape)
    return jnp.concatenate(
        [
            jnp.sum(jnp.where(first, wide, 0.0), axis=1, keepdims=True),
            jnp.sum(jnp.where(first, 0.0, wide), axis=1, keepdims=True),
        ],
        axis=1,
    )


def shifted_rows(x_ref, chunk):
    start = chunk * STRETCH
    if chunk == 0:
        extended = jnp.concatenate([jnp.zeros((8, LANES), F32), x_ref[0:STRETCH, :]], axis=0)
    else:
        extended = x_ref[start - 8 : start + STRETCH, :]
    return [extended[8:]] + [pltpu.roll(extended, s, 0)[8:] for s in (1, 2, 3)]


def convolved(shifted, w_ref, bias_ref):
    total = bias_ref[...] + w_ref[3:4, :] * shifted[0]
    for s in (1, 2, 3):
        total = total + w_ref[3 - s : 4 - s, :] * shifted[s]
    return total


def forward_kernel(
    x_ref, z_ref, gi_ref, b_ref, c_ref, bt_ref, dt_ref, cum_ref, row_ref,
    w_ref, bias_ref, skip_ref, gain_ref,
    scan_ref, state_ref, stat_ref,
    scores, squares, inners,
):
    group = pl.program_id(0)
    groups = pl.num_programs(0)

    @pl.when(group == 0)
    def _():
        squares[...] = jnp.zeros_like(squares)
        inners[...] = jnp.zeros_like(inners)
        for chunk in range(CHUNKS):
            rows = slice(chunk * STRETCH, (chunk + 1) * STRETCH)
            scores[chunk] = nt(c_ref[rows, :], b_ref[rows, :])

    lower = lax.broadcasted_iota(jnp.int32, (STRETCH, STRETCH), 0) >= lax.broadcasted_iota(
        jnp.int32, (STRETCH, STRETCH), 1
    )
    first = first_half((STRETCH, LANES))
    state = jnp.zeros((b_ref.shape[1], LANES), F32)
    for chunk in range(CHUNKS):
        rows = slice(chunk * STRETCH, (chunk + 1) * STRETCH)
        state_ref[0, chunk] = state
        conv = convolved(shifted_rows(x_ref, chunk), w_ref, bias_ref)
        mixed = conv * jax.nn.sigmoid(conv)
        cum = cum_ref[0, rows, :]
        cum_wide = spread(cum)
        last = cum_wide[STRETCH - 1 : STRETCH, :]
        dtx = mixed * spread(dt_ref[0, rows, :])
        dtx_low = dtx.astype(BF16)
        within = []
        for head in range(2):
            gap = cum[:, head : head + 1] - row_ref[0, head : head + 1, rows]
            decay = jnp.exp(jnp.where(lower, gap, -1e30))
            within.append(nn((scores[chunk] * decay).astype(BF16), dtx_low))
        carried = jnp.exp(cum_wide) * nn(c_ref[rows, :], state.astype(BF16))
        scanned = jnp.where(first, within[0], within[1]) + carried + skip_ref[...] * mixed
        scan_ref[rows, :] = scanned
        tail = (jnp.exp(last - cum_wide) * dtx).astype(BF16)
        state = jnp.exp(last) * state + nn(bt_ref[:, rows], tail)
        z = z_ref[rows, :]
        gated = scanned * (z * jax.nn.sigmoid(z))
        squares[rows, :] += gated * gated
        inners[rows, :] += gi_ref[rows, :] * gain_ref[...] * gated

    @pl.when(group == groups - 1)
    def _():
        stat_ref[...] = jnp.concatenate(
            [
                jnp.sum(squares[...], axis=1, keepdims=True),
                jnp.sum(inners[...], axis=1, keepdims=True),
            ],
            axis=1,
        )


def backward_kernel(
    x_ref, z_ref, gi_ref, scan_ref, stat_ref, b_ref, c_ref, ct_ref, dt_ref, cum_ref, row_ref,
    state_ref, w_ref, bias_ref, skip_ref, gain_ref,
    x_low_ref, ddt_ref, dcum_ref, param_ref, db_ref, dc_ref,
    scores, score_grad,
):
    group = pl.program_id(0)
    groups = pl.num_programs(0)

    @pl.when(group == 0)
    def _():
        score_grad[...] = jnp.zeros_like(score_grad)
        db_ref[...] = jnp.zeros_like(db_ref)
        dc_ref[...] = jnp.zeros_like(dc_ref)
        for chunk in range(CHUNKS):
            rows = slice(chunk * STRETCH, (chunk + 1) * STRETCH)
            scores[chunk] = nt(b_ref[rows, :], c_ref[rows, :])

    upper = lax.broadcasted_iota(jnp.int32, (STRETCH, STRETCH), 0) <= lax.broadcasted_iota(
        jnp.int32, (STRETCH, STRETCH), 1
    )
    first = first_half((STRETCH, LANES))
    at_end = lax.broadcasted_iota(jnp.int32, (STRETCH, LANES), 0) == STRETCH - 1
    state_grad = jnp.zeros((b_ref.shape[1], LANES), F32)
    following = jnp.zeros((8, LANES), F32)
    sums = [jnp.zeros((1, LANES), F32) for _ in range(6)]
    for chunk in reversed(range(CHUNKS)):
        rows = slice(chunk * STRETCH, (chunk + 1) * STRETCH)
        rms = stat_ref[rows, 0:1]
        inner = stat_ref[rows, 1:2]
        z = z_ref[rows, :]
        scanned = scan_ref[rows, :]
        gate = z * jax.nn.sigmoid(z)
        hat = scanned * gate * rms
        dy = rms * (gi_ref[rows, :] * gain_ref[...] - hat * inner) * gate

        shifted = shifted_rows(x_ref, chunk)
        conv = convolved(shifted, w_ref, bias_ref)
        sig = jax.nn.sigmoid(conv)
        mixed = conv * sig
        cum = cum_ref[0, rows, :]
        cum_wide = spread(cum)
        last = cum_wide[STRETCH - 1 : STRETCH, :]
        dt_wide = spread(dt_ref[0, rows, :])
        dtx = mixed * dt_wide
        dtx_low = dtx.astype(BF16)
        dy_low = dy.astype(BF16)
        dtx_back = []
        pair_grad = None
        for head in range(2):
            gap = row_ref[0, head : head + 1, rows] - cum[:, head : head + 1]
            decay = jnp.exp(jnp.where(upper, gap, -1e30))
            dtx_back.append(nn((scores[chunk] * decay).astype(BF16), dy_low))
            own = jnp.where(first if head == 0 else ~first, dy, 0.0).astype(BF16)
            term = nt(dtx_low, own) * decay
            pair_grad = term if pair_grad is None else pair_grad + term
        score_grad[chunk] += pair_grad
        state = state_ref[0, chunk]
        grow = jnp.exp(cum_wide)
        fall = jnp.exp(last - cum_wide)
        state_grad_low = state_grad.astype(BF16)
        arrival = fall * nn(b_ref[rows, :], state_grad_low)
        dtx_grad = jnp.where(first, dtx_back[0], dtx_back[1]) + arrival
        extra = jnp.sum(dtx_low.astype(F32) * arrival, axis=0, keepdims=True) + jnp.exp(last) * jnp.sum(
            state * state_grad, axis=0, keepdims=True
        )
        dy_grown = (grow * dy).astype(BF16)
        db_ref[rows, :] += nt((fall * dtx).astype(BF16), state_grad_low)
        dc_ref[rows, :] += nt(dy_grown, state.astype(BF16))
        state_grad = jnp.exp(last) * state_grad + nn(ct_ref[:, rows], dy_grown)

        balance = dy_low.astype(F32) * (scanned - skip_ref[...] * mixed) - (
            dtx_low.astype(F32) * dtx_grad
        )
        dcum_ref[0, rows, :] = head_sums(balance + jnp.where(at_end, extra, 0.0))
        ddt_ref[0, rows, :] = head_sums(mixed * dtx_grad)
        conv_grad = (dt_wide * dtx_grad + skip_ref[...] * dy) * (sig * (1.0 + conv * (1.0 - sig)))
        extended = jnp.concatenate([conv_grad, following], axis=0)
        following = conv_grad[0:8]
        back = w_ref[3:4, :] * conv_grad
        for s in (1, 2, 3):
            back = back + w_ref[3 - s : 4 - s, :] * pltpu.roll(extended, STRETCH + 8 - s, 0)[:STRETCH]
        x_low_ref[rows, :] = back.astype(BF16)
        parts = [conv_grad * shifted[3 - k] for k in range(4)] + [conv_grad, dy * mixed]
        sums = [old + jnp.sum(new, axis=0, keepdims=True) for old, new in zip(sums, parts)]
    param_ref[...] = jnp.concatenate(sums + [jnp.zeros((2, LANES), F32)], axis=0)

    @pl.when(group == groups - 1)
    def _():
        for chunk in range(CHUNKS):
            rows = slice(chunk * STRETCH, (chunk + 1) * STRETCH)
            grad = score_grad[chunk].astype(BF16)
            db_ref[rows, :] += nn(grad, c_ref[rows, :])
            dc_ref[rows, :] += tn(grad, b_ref[rows, :])


def wide(rows=SEQ_LEN):
    return pl.BlockSpec((rows, LANES), lambda g: (0, g))


def fixed(*shape):
    return pl.BlockSpec(shape, lambda g: (0,) * len(shape))


def grouped(*shape):
    return pl.BlockSpec((1,) + shape, lambda g: (g,) + (0,) * len(shape))


def by_group(columns):
    rows, heads = columns.shape
    return columns.reshape(rows, heads // 2, 2).transpose(1, 0, 2)


def from_groups(pairs):
    groups, rows, _ = pairs.shape
    return pairs.transpose(1, 0, 2).reshape(rows, groups * 2)


def scan_forward(x_pre, z_pre, gate_in, b_low, c_low, dt3, cum3, row3, x_conv, x_bias, skip, gain):
    channels = x_pre.shape[1]
    groups = channels // LANES
    n = b_low.shape[1]
    return pl.pallas_call(
        forward_kernel,
        grid=(groups,),
        in_specs=[
            wide(), wide(), wide(), fixed(SEQ_LEN, n), fixed(SEQ_LEN, n), fixed(n, SEQ_LEN),
            grouped(SEQ_LEN, 2), grouped(SEQ_LEN, 2), grouped(2, SEQ_LEN),
            wide(4), wide(1), wide(1), wide(1),
        ],
        out_specs=[wide(), grouped(CHUNKS, n, LANES), fixed(SEQ_LEN, 2)],
        out_shape=[
            jax.ShapeDtypeStruct((SEQ_LEN, channels), F32),
            jax.ShapeDtypeStruct((groups, CHUNKS, n, LANES), F32),
            jax.ShapeDtypeStruct((SEQ_LEN, 2), F32),
        ],
        scratch_shapes=[
            pltpu.VMEM((CHUNKS, STRETCH, STRETCH), F32),
            pltpu.VMEM((SEQ_LEN, LANES), F32),
            pltpu.VMEM((SEQ_LEN, LANES), F32),
        ],
        compiler_params=pltpu.CompilerParams(vmem_limit_bytes=32 * 1024 * 1024),
        cost_estimate=pl.CostEstimate(
            flops=2 * 10**9, bytes_accessed=24 * 2**20, transcendentals=groups * 600000
        ),
    )(x_pre, z_pre, gate_in, b_low, c_low, b_low.T, dt3, cum3, row3, x_conv, x_bias, skip, gain)


def scan_backward(
    x_pre, z_pre, gate_in, scanned, stats, b_low, c_low, dt3, cum3, row3, states,
    x_conv, x_bias, skip, gain,
):
    channels = x_pre.shape[1]
    groups = channels // LANES
    n = b_low.shape[1]
    return pl.pallas_call(
        backward_kernel,
        grid=(groups,),
        in_specs=[
            wide(), wide(), wide(), wide(), fixed(SEQ_LEN, 2),
            fixed(SEQ_LEN, n), fixed(SEQ_LEN, n), fixed(n, SEQ_LEN),
            grouped(SEQ_LEN, 2), grouped(SEQ_LEN, 2), grouped(2, SEQ_LEN),
            grouped(CHUNKS, n, LANES), wide(4), wide(1), wide(1), wide(1),
        ],
        out_specs=[
            wide(), grouped(SEQ_LEN, 2), grouped(SEQ_LEN, 2), wide(8),
            fixed(SEQ_LEN, n), fixed(SEQ_LEN, n),
        ],
        out_shape=[
            jax.ShapeDtypeStruct((SEQ_LEN, channels), BF16),
            jax.ShapeDtypeStruct((groups, SEQ_LEN, 2), F32),
            jax.ShapeDtypeStruct((groups, SEQ_LEN, 2), F32),
            jax.ShapeDtypeStruct((8, channels), F32),
            jax.ShapeDtypeStruct((SEQ_LEN, n), F32),
            jax.ShapeDtypeStruct((SEQ_LEN, n), F32),
        ],
        scratch_shapes=[
            pltpu.VMEM((CHUNKS, STRETCH, STRETCH), F32),
            pltpu.VMEM((CHUNKS, STRETCH, STRETCH), F32),
        ],
        compiler_params=pltpu.CompilerParams(vmem_limit_bytes=32 * 1024 * 1024),
        cost_estimate=pl.CostEstimate(
            flops=60 * 10**9, bytes_accessed=200 * 2**20, transcendentals=groups * 800000
        ),
    )(
        x_pre, z_pre, gate_in, scanned, stats, b_low, c_low, c_low.T, dt3, cum3, row3, states,
        x_conv, x_bias, skip, gain,
    )


def over_tensor(value):
    if lax.axis_size("tensor") == 2:
        return value + lax.ppermute(value, "tensor", [(0, 1), (1, 0)])
    return lax.psum(value, "tensor")


def per_device(
    tokens, norm_gain, z_proj, x_proj, dt_proj, bc_proj, x_conv, x_conv_bias, bc_conv,
    bc_conv_bias, dt_bias, a_log, d_skip, gate_gain, out_proj, cotangent,
):
    heads = dt_proj.shape[1]
    channels = x_proj.shape[1]
    head_dim = channels // heads
    width = tokens.shape[1]
    hidden = tokens.astype(F32)
    inv_rms = lax.rsqrt(jnp.mean(hidden * hidden, axis=1, keepdims=True) + EPS)
    normed = hidden * inv_rms
    normed_in = (normed * norm_gain).astype(BF16)
    bc_pre = nn(normed_in, bc_proj)
    dt_pre = nn(normed_in, dt_proj)
    z_pre = nn(normed_in, z_proj)
    x_pre = nn(normed_in, x_proj)
    gate_in_grad = nt(cotangent, out_proj)

    bc_mixed, bc_pull = jax.vjp(causal_conv, bc_pre, bc_conv, bc_conv_bias)
    bc_mixed_low = bc_mixed.astype(BF16)
    state_size = bc_mixed.shape[1] // 2
    b_low, c_low = bc_mixed_low[:, :state_size], bc_mixed_low[:, state_size:]
    step_dt = jax.nn.softplus(dt_pre + dt_bias)
    rate = -jnp.exp(a_log)
    places = jnp.arange(STRETCH)
    lower = (places[:, None] >= places[None, :]).astype(F32)
    cum = jnp.einsum(
        "ij,bjh->bih", lower, (step_dt * rate).reshape(CHUNKS, STRETCH, heads), precision=HIGH
    ).reshape(SEQ_LEN, heads)
    dt3, cum3 = by_group(step_dt), by_group(cum)
    row3 = cum.T.reshape(heads // 2, 2, SEQ_LEN)
    skip = jnp.repeat(d_skip, head_dim)[None, :]
    bias = x_conv_bias[None, :]
    gain = gate_gain[None, :]
    scanned, states, stats = scan_forward(
        x_pre, z_pre, gate_in_grad, b_low, c_low, dt3, cum3, row3, x_conv, bias, skip, gain
    )
    stats = over_tensor(stats)
    gate_rms = lax.rsqrt(stats[:, 0:1] / INNER + EPS)
    inner_mean = stats[:, 1:2] * gate_rms / INNER

    sig_z = jax.nn.sigmoid(z_pre)
    silu_z = z_pre * sig_z
    gate_hat = scanned * silu_z * gate_rms
    gate_out = (gate_hat * gate_gain).astype(BF16)
    gate_gain_grad = jnp.sum(gate_in_grad * gate_hat, axis=0)
    gated_grad = gate_rms * (gate_in_grad * gate_gain - gate_hat * inner_mean)
    z_low = (gated_grad * scanned * (sig_z * (1.0 + z_pre * (1.0 - sig_z)))).astype(BF16)
    out_proj_grad = tn(gate_out, cotangent).astype(BF16)
    z_proj_part = tn(normed_in, z_low)
    out_proj_grad, z_proj_grad = lax.psum((out_proj_grad, z_proj_part.astype(BF16)), "dp")

    x_low, ddt3, dcum3, params, db, dc = scan_backward(
        x_pre, z_pre, gate_in_grad, scanned, jnp.concatenate([gate_rms, inner_mean], axis=1),
        b_low, c_low, dt3, cum3, row3, states, x_conv, bias, skip, gain,
    )
    branch = over_tensor(nn(gate_out, out_proj).astype(BF16)).astype(F32)
    mixed = (hidden + branch).astype(BF16)

    bc_grad, bc_conv_grad, bc_conv_bias_grad = bc_pull(jnp.concatenate([db, dc], axis=1))
    bc_low = bc_grad.astype(BF16)
    decay_grad = jnp.einsum(
        "ji,bjh->bih", lower, from_groups(dcum3).reshape(CHUNKS, STRETCH, heads), precision=HIGH
    ).reshape(SEQ_LEN, heads)
    dt_grad = (decay_grad * rate + from_groups(ddt3)) * jax.nn.sigmoid(dt_pre + dt_bias)
    a_log_grad = jnp.sum(decay_grad * step_dt, axis=0) * rate
    dt_bias_grad = jnp.sum(dt_grad, axis=0)
    dt_low = dt_grad.astype(BF16)
    x_proj_part = tn(normed_in, x_low)
    bc_proj_part = tn(normed_in, bc_low)
    dt_proj_part = tn(normed_in, dt_low)
    norm_part = (
        jnp.sum(z_proj_part * z_proj.astype(F32), axis=1)
        + jnp.sum(x_proj_part * x_proj.astype(F32), axis=1)
        + jnp.sum(bc_proj_part * bc_proj.astype(F32), axis=1)
        + jnp.sum(dt_proj_part * dt_proj.astype(F32), axis=1)
    ) / norm_gain
    bc_proj_part = over_tensor(bc_proj_part.astype(BF16))
    shared = over_tensor(
        jnp.concatenate([norm_part, bc_conv_grad.reshape(-1), bc_conv_bias_grad])
    )
    own = [
        dt_proj_part, params[0:4], params[4], dt_bias_grad, a_log_grad,
        jnp.sum(params[5].reshape(heads, head_dim), axis=1), gate_gain_grad,
    ]
    pieces = [shared] + [part.reshape(-1) for part in own]
    count = sum(piece.size for piece in pieces)
    total = -(-count // 2048) * 2048
    small = jnp.concatenate(pieces + [jnp.zeros((total - count,), F32)]).reshape(-1, 128)
    x_part, bc_part, small, out_proj_grad, z_proj_grad = lax.optimization_barrier(
        (x_proj_part.astype(BF16), bc_proj_part, small.astype(BF16), out_proj_grad, z_proj_grad)
    )
    x_proj_grad, bc_proj_grad, small = lax.psum((x_part, bc_part, small), "dp")

    summed = nt(z_low, z_proj) + nt(x_low, x_proj) + nt(dt_low, dt_proj) + nt(bc_low, bc_proj)
    full_grad = over_tensor(summed.astype(BF16)).astype(F32)
    scaled = full_grad * norm_gain
    full_back = inv_rms * (scaled - normed * jnp.mean(scaled * normed, axis=1, keepdims=True))
    tokens_grad = (full_back + cotangent.astype(F32)).astype(BF16)

    flat = small.reshape(-1).astype(F32)
    taken = []
    start = 0
    shapes = [(width,), bc_conv.shape, bc_conv_bias.shape] + [part.shape for part in own]
    for shape in shapes:
        size = 1
        for dim in shape:
            size *= dim
        taken.append(flat[start : start + size].reshape(shape))
        start += size
    (
        norm_gain_grad, bc_conv_grad, bc_conv_bias_grad, dt_proj_grad, x_conv_grad,
        x_conv_bias_grad, dt_bias_grad, a_log_grad, d_skip_grad, gate_gain_grad,
    ) = taken
    return (
        mixed,
        tokens_grad,
        norm_gain_grad,
        z_proj_grad.astype(F32),
        x_proj_grad.astype(F32),
        dt_proj_grad,
        bc_proj_grad.astype(F32),
        x_conv_grad,
        x_conv_bias_grad,
        bc_conv_grad,
        bc_conv_bias_grad,
        dt_bias_grad,
        a_log_grad,
        d_skip_grad,
        gate_gain_grad,
        out_proj_grad.astype(F32),
    )


def solution(mesh):
    placed = (
        P("dp", None),
        P(),
        P(None, "tensor"),
        P(None, "tensor"),
        P(None, "tensor"),
        P(),
        P(None, "tensor"),
        P("tensor"),
        P(),
        P(),
        P("tensor"),
        P("tensor"),
        P("tensor"),
        P("tensor"),
        P("tensor", None),
        P("dp", None),
    )
    return jax.shard_map(
        per_device,
        mesh=mesh,
        in_specs=placed,
        out_specs=(
            P("dp", None),
            P("dp", None),
            P(),
            P(None, "tensor"),
            P(None, "tensor"),
            P(None, "tensor"),
            P(),
            P(None, "tensor"),
            P("tensor"),
            P(),
            P(),
            P("tensor"),
            P("tensor"),
            P("tensor"),
            P("tensor"),
            P("tensor", None),
        ),
        check_vma=False,
    )
```
